1024 devices in a mesh: dp: 4 (over z_hi), expert: 64 (over z_lo, x, core), mp: 4 (over y).
Axes of the slice: x: 4, y: 4, z: 32 (z_hi: 4, z_lo: 8; z = z_hi * 8 + z_lo), core: 2. Of those that a mesh axis runs over, the one named last changes fastest.
Arguments:
- x_rows: bfloat16 [32768, 3072], P(('dp', 'expert')), may hold values from -6 to 6, as said below
- dy_rows: bfloat16 [32768, 3072], P(('dp', 'expert')), may hold values from -1.5 to 1.5, as said below
- w_in: bfloat16 [64, 3072, 2, 1344], P('expert', None, None, 'mp'), may hold values from -0.109375 to 0.109375
- w_out: bfloat16 [64, 3072, 1344], P('expert', None, 'mp'), may hold values from -0.078125 to 0.078125
- counts: int32 [256, 64], P(('dp', 'expert')), may hold values from 0 to 2, as said below
- assign: int32 [1024, 4], P(('dp', 'expert')), may hold values from 0 to 15, as said below
Outputs:
- grad_w_in: bfloat16 [64, 3072, 2, 1344], P('expert', 'dp', None, 'mp')
- grad_w_out: bfloat16 [64, 3072, 1344], P('expert', 'dp', 'mp')
- grad_tokens: bfloat16 [1024, 3072], P(('dp', 'expert'), 'mp')
The draws below stay inside these ranges and needn't reach their ends.
Inputs may be any that keep to these rules, and one draw needn't show every extreme that they name: counts[(g, u), s] is the number of tokens of owner s of group g that name expert e = u // 4 in assign, equal for the slices of one expert; it is at most 2, and 2 is reached in every group. `assign`: each token names 4 different experts; no owner names one expert for more than 2 of its tokens. `x_rows`: the 4 slices of one expert in one group keep equal copies of the same rows. `dy_rows`: the 4 slices of one expert in one group keep equal copies of the same rows.
All inputs are finite; a program needn't handle non-finite values.
Results may differ from the reference program's by a relative error of at most 0.018.
Values may be sent and summed in bfloat16 or wider, within the bound.
A program may use at most 64 MiB of HBM per device.

```python
import jax
import jax.numpy as jnp
from jax import lax

D = 3072
TOK = 4
EXPERTS = 16
TOP = 4
SLICES = 4
OWNERS = 64
SLICE_FF = 1344
FF_EXP = 5376
HOT = 4
CAP = 2
ROWS = 128
N_DP = 4
N_EXPERT = 64


def expert_order(group_key):
    return jax.random.permutation(group_key, EXPERTS)


def token_columns(column_key):
    return jax.random.permutation(column_key, TOP)


def route_tables(base_key):
    owner_total = N_DP * OWNERS
    route_total = TOK * TOP
    cold_count = EXPERTS - HOT
    spare_rows = route_total - HOT * CAP
    group_keys = jax.random.split(jax.random.fold_in(base_key, 11), N_DP)
    owner_keys = jax.random.split(jax.random.fold_in(base_key, 12), owner_total)
    rank_order = jax.vmap(expert_order)(group_keys)

    def owner_counts(owner_key):
        chosen = (jax.random.permutation(owner_key, cold_count * CAP) < spare_rows).astype(jnp.int32)
        cold_rows = jnp.sum(chosen.reshape(cold_count, CAP), axis=1)
        return jnp.concatenate([jnp.full((HOT,), CAP, jnp.int32), cold_rows])
    by_rank = jax.vmap(owner_counts)(owner_keys).reshape(N_DP, OWNERS, EXPERTS)
    rank_of = jnp.argsort(rank_order, axis=1, stable=True).astype(jnp.int32)
    per_expert = jnp.take_along_axis(by_rank, jnp.broadcast_to(rank_of[:, None, :], by_rank.shape), axis=2)

    def owner_routes(count_row, owner_key):
        bounds = jnp.cumsum(count_row)
        ordered = jnp.searchsorted(bounds, jnp.arange(route_total, dtype=jnp.int32), side='right').astype(jnp.int32)
        routes = ordered.reshape(TOP, TOK).T
        token_order = jax.random.permutation(jax.random.fold_in(owner_key, 1), TOK)
        column_keys = jax.random.split(jax.random.fold_in(owner_key, 2), TOK)
        column_order = jax.vmap(token_columns)(column_keys)
        return jnp.take_along_axis(routes[token_order], column_order, axis=1)
    routes_all = jax.vmap(owner_routes)(per_expert.reshape(owner_total, EXPERTS), owner_keys)
    assign = routes_all.reshape(owner_total * TOK, TOP).astype(jnp.int32)
    by_expert = jnp.transpose(per_expert, (0, 2, 1))
    counts = jnp.repeat(by_expert, SLICES, axis=1).reshape(N_DP * N_EXPERT, OWNERS).astype(jnp.int32)
    return (assign, counts)


def slice_copies(key, scale, bound):
    base = jnp.clip(scale * jax.random.normal(key, (N_DP, EXPERTS, 1, ROWS, D), jnp.float32), -bound, bound)
    tiled = jnp.broadcast_to(base, (N_DP, EXPERTS, SLICES, ROWS, D))
    return tiled.reshape(N_DP * N_EXPERT * ROWS, D).astype(jnp.bfloat16)


def draw_x_rows(key, part):
    key = jax.random.fold_in(key, 21)
    return slice_copies(key, 1.0, 6.0)


def draw_dy_rows(key, part):
    key = jax.random.fold_in(key, 22)
    return slice_copies(key, 0.25, 1.5)


def draw_counts(key, part):
    return route_tables(key)[1]


def draw_assign(key, part):
    return route_tables(key)[0]


def level_of(own_key, dims, cuts, smallest, top_value):
    def one(axis_at, parts):
        heights = jax.random.uniform(jax.random.fold_in(jax.random.fold_in(own_key, 6), axis_at), (parts,), jnp.float32, smallest / len(cuts), top_value / len(cuts))
        return jnp.repeat(jnp.exp(heights), dims[axis_at] // parts).reshape((-1,) + (1,) * (len(dims) - axis_at - 1))

    level = one(*cuts[0])
    for cut in cuts[1:]:
        level = level * one(*cut)
    return level


def bell_draw(key, shape, scale, reach, cuts=(), kind=jnp.bfloat16):
    values = scale * jax.random.normal(key, shape, jnp.float32)
    if cuts:
        values = values * level_of(key, shape, cuts, -0.22, 0.18)
    return jnp.clip(values, -reach, reach).astype(kind)


def setup_inputs(seed: int = 0) -> dict:
    streams_of = jax.random.split(jax.random.key(seed), 7)
    return {
        "x_rows": draw_x_rows(jax.random.fold_in(streams_of[6], 71), 0),
        "dy_rows": draw_dy_rows(jax.random.fold_in(streams_of[6], 71), 0),
        "w_in": bell_draw(streams_of[2], (N_EXPERT, D, 2, SLICE_FF), D ** -0.5, 0.109375, ((0, 64), (3, 4))),
        "w_out": bell_draw(streams_of[3], (N_EXPERT, D, SLICE_FF), FF_EXP ** -0.5, 0.078125, ((0, 64), (2, 4))),
        "counts": draw_counts(jax.random.fold_in(streams_of[6], 71), 0),
        "assign": draw_assign(jax.random.fold_in(streams_of[6], 71), 0),
    }


def expert_rows(x_block, dy_block, w_flat, w_down, live_mask):
    preact = jnp.dot(x_block, w_flat, preferred_element_type=jnp.float32)
    gate_pre = preact[:, :SLICE_FF]
    up_pre = preact[:, SLICE_FF:]
    sigmoid_gate = jax.nn.sigmoid(gate_pre)
    hidden = (live_mask * gate_pre * sigmoid_gate * up_pre).astype(jnp.bfloat16)
    grad_hidden = jnp.dot(dy_block, w_down, preferred_element_type=jnp.float32)
    grad_gate = live_mask * grad_hidden * up_pre * sigmoid_gate * (1.0 + gate_pre * (1.0 - sigmoid_gate))
    grad_up = live_mask * grad_hidden * gate_pre * sigmoid_gate
    grad_pre = jnp.concatenate([grad_gate, grad_up], axis=1).astype(jnp.bfloat16)
    row_parts = lax.dot_general(grad_pre, w_flat, (((1,), (1,)), ((), ())), preferred_element_type=jnp.float32).astype(jnp.bfloat16)
    term_in = lax.dot_general(x_block, grad_pre, (((0,), (0,)), ((), ())), preferred_element_type=jnp.float32).astype(jnp.bfloat16)
    term_out = lax.dot_general(dy_block, hidden, (((0,), (0,)), ((), ())), preferred_element_type=jnp.float32).astype(jnp.bfloat16)
    return row_parts, term_in, term_out


def reference(x_rows, dy_rows, w_in, w_out, counts, assign):
    live_total = jnp.sum(counts, axis=1).reshape(N_DP, N_EXPERT)
    x_groups = x_rows.reshape(N_DP, N_EXPERT, ROWS, D)
    dy_groups = dy_rows.reshape(N_DP, N_EXPERT, ROWS, D)
    slot_index = jnp.arange(ROWS, dtype=jnp.int32)

    def per_slice(slice_index):
        w_flat = w_in[slice_index].reshape(D, 2 * SLICE_FF)
        w_down = w_out[slice_index]
        row_list = []
        total_in = jnp.zeros((D, 2 * SLICE_FF), jnp.float32)
        total_out = jnp.zeros((D, SLICE_FF), jnp.float32)
        for replica in range(N_DP):
            live_mask = (slot_index < live_total[replica, slice_index]).astype(jnp.float32)[:, None]
            row_parts, term_in, term_out = expert_rows(x_groups[replica, slice_index], dy_groups[replica, slice_index], w_flat, w_down, live_mask)
            row_list.append(row_parts)
            total_in = total_in + lax.optimization_barrier(term_in).astype(jnp.float32)
            total_out = total_out + lax.optimization_barrier(term_out).astype(jnp.float32)
        grad_in = total_in.astype(jnp.bfloat16).reshape(D, 2, SLICE_FF)
        return jnp.stack(row_list), grad_in, total_out.astype(jnp.bfloat16)

    all_rows, grad_w_in, grad_w_out = lax.map(per_slice, jnp.arange(N_EXPERT, dtype=jnp.int32))
    count_cube = counts.reshape(N_DP, N_EXPERT, OWNERS)[:, ::SLICES]
    offsets = (jnp.cumsum(count_cube, axis=2) - count_cube).astype(jnp.int32)
    flat_routes = assign.reshape(N_DP, OWNERS, TOK * TOP).astype(jnp.int32)
    same_expert = flat_routes[:, :, :, None] == flat_routes[:, :, None, :]
    token_of = jnp.arange(TOK * TOP, dtype=jnp.int32) // TOP
    earlier = token_of[None, :] < token_of[:, None]
    route_rank = jnp.sum((same_expert & earlier[None, None]).astype(jnp.int32), axis=3)
    replica_index = jnp.arange(N_DP, dtype=jnp.int32)[:, None, None]
    owner_index = jnp.arange(OWNERS, dtype=jnp.int32)[None, :, None]
    slot_start = offsets[replica_index, flat_routes, owner_index]
    slice_ids = jnp.arange(SLICES, dtype=jnp.int32)[None, None, None, :]
    unit = flat_routes[..., None] * SLICES + slice_ids
    row_index = ((unit * N_DP + replica_index[..., None]) * ROWS + (slot_start + route_rank)[..., None]).astype(jnp.int32)
    picked = all_rows.reshape(N_EXPERT * N_DP * ROWS, D)[row_index]
    summed = jnp.sum(picked.astype(jnp.float32).reshape(N_DP, OWNERS, TOK, TOP * SLICES, D), axis=3)
    grad_tokens = summed.astype(jnp.bfloat16).reshape(N_DP * OWNERS * TOK, D)
    return grad_w_in, grad_w_out, grad_tokens
```

```python
import jax
import jax.numpy as jnp
from jax import lax
from jax.experimental import pallas as pl
from jax.experimental.pallas import tpu as pltpu
from jax.sharding import PartitionSpec as P

MESH = pl.DeviceIdType.MESH
N_DP = 4
N_MP = 4
SLICES = 4
EXPERTS = 16
SLOTS = 128
QUARTERS = 4

ROUNDS = (
    ((3, 0), (1, 3)),
    ((3, 1), (1, 2)),
    ((3, 2), (1, 1)),
    ((3, 3), (1, 0)),
    ((2, 0), (2, 3)),
    ((2, 1), (2, 2)),
)
CHUNKS = tuple(chunk for pair in ROUNDS for chunk in pair)


def fused_kernel(
    x_ref, dy_ref, w_ref, wo_ref, counts_ref, assign_ref,
    gin_ref, gout_ref, gtok_ref,
    rows, w_in, w_out, acc, gpt, hdt, parts, got_f, sums, got_y, sent_t, got_t, comb,
    load_sem, zs, zr, xs, xr, ys, yr, cs, cr, fs, fr, ms, mr, ts, tr,
):
    units = w_out.shape[0]
    model = w_in.shape[1]
    quarter = model // QUARTERS
    g = lax.axis_index("dp")
    u = lax.axis_index("expert")
    m = lax.axis_index("mp")
    core = lax.rem(u, 2)
    half_x = lax.rem(lax.div(u, 2), 2)
    f = lax.rem(u, SLICES)
    e = lax.div(u, SLICES)
    plane_f = lax.div(lax.div(u, 8), 2)
    flip_core = 1 - 2 * core
    flip_x = 2 - 4 * half_x
    f_shift = (flip_core, flip_x, flip_core + flip_x)
    left_g, right_g = lax.rem(g + N_DP - 1, N_DP), lax.rem(g + 1, N_DP)
    m_at = [lax.rem(m + step, N_MP) for step in range(N_MP)]

    def loads():
        out = []
        for q in range(QUARTERS):
            cols = pl.ds(q * quarter, quarter)
            out.append(pltpu.make_async_copy(dy_ref.at[:, cols], rows.at[1, 0, q], load_sem.at[q]))
            out.append(pltpu.make_async_copy(x_ref.at[:, cols], rows.at[0, 0, q], load_sem.at[4 + q]))
        out.append(pltpu.make_async_copy(w_ref, w_in, load_sem.at[8]))
        out.append(pltpu.make_async_copy(wo_ref, w_out, load_sem.at[9]))
        return out

    local = loads()
    for copy in local:
        copy.start()

    barrier = pltpu.get_barrier_semaphore()

    def hello(where):
        pl.semaphore_signal(barrier, inc=1, device_id=where, device_id_type=MESH)

    hello({"dp": left_g})
    hello({"dp": right_g})
    for shift in f_shift:
        hello({"expert": u + shift})
    for step in range(1, N_MP):
        hello({"mp": m_at[step]})
    for expert in range(EXPERTS):
        source = expert * SLICES + plane_f

        @pl.when(source != u)
        def _():
            hello({"expert": source})

    own_target = (plane_f == f).astype(jnp.int32)

    counts = counts_ref[...].astype(jnp.float32)
    live_rows = jnp.sum(counts, axis=1, keepdims=True)
    row_at = lax.broadcasted_iota(jnp.int32, (SLOTS, 1), 0)
    live = row_at.astype(jnp.float32) < live_rows
    for q in range(QUARTERS):
        local[2 * q].wait()
        dy = rows[1, 0, q]
        rows[1, 0, q] = jnp.where(live, dy, jnp.zeros_like(dy))
        local[2 * q + 1].wait()

    pl.semaphore_wait(barrier, 8 + EXPERTS - own_target)

    def rcopy(src, dst, send, recv, where):
        return pltpu.make_async_remote_copy(
            src_ref=src, dst_ref=dst, send_sem=send, recv_sem=recv, device_id=where, device_id_type=MESH
        )

    def at(kind, distance, q, start, size):
        return rows.at[kind, distance, q, pl.ds(pl.multiple_of(start, 16), size)]

    own_16 = m * 32 + half_x * 16
    pair_16 = m * 32 + (1 - half_x) * 16

    def z_copy(i):
        distance, q = CHUNKS[i]
        dst = at(core, distance, q, own_16, 16)
        if distance == 3:
            return rcopy(at(core, 0, q, own_16, 16), dst, zs.at[i], zr.at[i], {"dp": right_g})
        if distance == 1:
            return rcopy(at(core, 0, q, own_16, 16), dst, zs.at[i], zr.at[i], {"dp": left_g})
        if q < 2:
            return rcopy(at(core, 3, q, own_16, 16), dst, zs.at[i], zr.at[i], {"dp": right_g})
        return rcopy(at(core, 1, q, own_16, 16), dst, zs.at[i], zr.at[i], {"dp": left_g})

    def x_copy(i, start):
        d, q = CHUNKS[i]
        block = at(core, d, q, start, 16)
        return rcopy(block, block, xs.at[i], xr.at[i], {"expert": u + flip_x})

    def y_copy(i, way, block_m):
        d, q = CHUNKS[i]
        block = at(core, d, q, block_m * 32, 32)
        j = 4 * i + way
        return rcopy(block, block, ys.at[j], yr.at[j], {"mp": m_at[1] if way == 0 else m_at[3]})

    def y_forward(i, way, block_m):
        d, q = CHUNKS[i]
        block = at(core, d, q, block_m * 32 + 16 * way, 16)
        j = 4 * i + 2 + way
        return rcopy(block, block, ys.at[j], yr.at[j], {"mp": m_at[1] if way == 0 else m_at[3]})

    def c_copy(i, kind):
        d, q = CHUNKS[i]
        block = rows.at[kind, d, q]
        return rcopy(block, block, cs.at[i], cr.at[i], {"expert": u + flip_core})

    for i in range(8):
        z_copy(i).start()

    def stage_z(k):
        for i in (2 * k, 2 * k + 1):
            z_copy(i).wait_recv()
            if k < 2:
                z_copy(8 + i).start()
            x_copy(i, own_16).start()

    def stage_x(k):
        for i in (2 * k, 2 * k + 1):
            x_copy(i, pair_16).wait_recv()
            for way in range(2):
                y_copy(i, way, m).start()

    def stage_y(k):
        for i in (2 * k, 2 * k + 1):
            y_copy(i, 0, m_at[3]).wait_recv()
            y_forward(i, 0, m_at[3]).start()
            y_copy(i, 1, m_at[1]).wait_recv()
            y_forward(i, 1, m_at[1]).start()

    def stage_f(k):
        for i in (2 * k, 2 * k + 1):
            for way in range(2):
                y_forward(i, way, m_at[2]).wait_recv()
            c_copy(i, core).start()

    def multiply(d, q):
        cols = pl.ds(q * quarter, quarter)
        pre = lax.dot_general(
            w_in[:, cols], rows[0, d, q], (((1,), (1,)), ((), ())), preferred_element_type=jnp.float32
        )
        grad = lax.dot_general(
            w_out[:, cols], rows[1, d, q], (((1,), (1,)), ((), ())), preferred_element_type=jnp.float32
        )
        return pre, grad

    def stage_c(k):
        for i in (2 * k, 2 * k + 1):
            c_copy(i, 1 - core).wait_recv()
            d, q = CHUNKS[i]
            pre, grad = multiply(d, q)
            first = i < 2 or i == 8
            if first:
                acc[d, : 2 * units] = pre
                acc[d, 2 * units :] = grad
            else:
                acc[d, : 2 * units] += pre
                acc[d, 2 * units :] += grad

    def activate(d):
        gate = acc[d, :units]
        up = acc[d, units : 2 * units]
        grad = acc[d, 2 * units :]
        sigmoid = jax.nn.sigmoid(gate)
        lanes = pl.ds(d * SLOTS, SLOTS)
        hdt[:, lanes] = (gate * sigmoid * up).astype(jnp.bfloat16)
        gpt[:units, lanes] = (grad * up * sigmoid * (1.0 + gate * (1.0 - sigmoid))).astype(jnp.bfloat16)
        gpt[units:, lanes] = (grad * gate * sigmoid).astype(jnp.bfloat16)

    local[8].wait()
    local[9].wait()
    for q in range(QUARTERS):
        pre, grad = multiply(0, q)
        if q == 0:
            acc[0, : 2 * units] = pre
            acc[0, 2 * units :] = grad
        else:
            acc[0, : 2 * units] += pre
            acc[0, 2 * units :] += grad
    activate(0)

    place = lax.broadcasted_iota(jnp.int32, (SLOTS, 1), 0)
    owner = jnp.right_shift(lax.broadcasted_iota(jnp.int32, (SLOTS, 64), 0), 1)
    other = lax.broadcasted_iota(jnp.int32, (SLOTS, 64), 1)
    spread = jnp.broadcast_to(counts, (SLOTS, 64))
    zero = jnp.zeros_like(spread)
    start = jnp.sum(jnp.where(other < owner, spread, zero), axis=1, keepdims=True)
    held = jnp.sum(jnp.where(other == owner, spread, zero), axis=1, keepdims=True)
    rank = jnp.bitwise_and(place, 1).astype(jnp.float32)
    wanted = jnp.where(rank < held, start + rank, -1.0)
    slot_at = lax.broadcasted_iota(jnp.int32, (SLOTS, SLOTS), 1).astype(jnp.float32)
    order = jnp.where(slot_at == wanted, 1.0, 0.0).astype(jnp.bfloat16)
    ordered = lax.dot_general(
        order, gpt[:, :SLOTS], (((1,), (1,)), ((), ())), preferred_element_type=jnp.float32
    ).astype(jnp.bfloat16)
    for q in range(QUARTERS):
        cols = pl.ds(q * quarter, quarter)
        parts[:, cols] = jnp.dot(ordered, w_in[:, cols], preferred_element_type=jnp.float32).astype(
            jnp.bfloat16
        )

    def f_copy(j):
        target = f + f_shift[j]
        src = parts.at[pl.ds(pl.multiple_of(target * 32, 32), 32)]
        return rcopy(src, got_f.at[j], fs.at[j], fr.at[j], {"expert": u + f_shift[j]})

    for j in range(3):
        f_copy(j).start()

    def sum_slices():
        for j in range(3):
            f_copy(j).wait_recv()
        mine = pl.ds(pl.multiple_of(f * 32, 32), 32)
        for q in range(QUARTERS):
            cols = pl.ds(q * quarter, quarter)
            total = parts[mine, cols].astype(jnp.float32)
            for j in range(3):
                total = total + got_f[j, :, cols].astype(jnp.float32)
            sums[q] = total.astype(jnp.bfloat16)
        for step in range(1, N_MP):
            m_copy(step).start()

    def m_copy(step):
        return rcopy(
            sums.at[m_at[step]], got_y.at[step - 1], ms.at[step - 1], mr.at[step - 1], {"mp": m_at[step]}
        )

    def token_copy(i):
        return rcopy(sent_t.at[i], got_t.at[e], ts.at[i], tr.at[e], {"expert": 16 * f + i})

    def token_arrival(expert):
        return rcopy(
            sent_t.at[expert], got_t.at[expert], ts.at[expert], tr.at[expert], {"expert": u}
        )

    def token_local(i):
        return pltpu.make_async_copy(sent_t.at[i], got_t.at[e], tr.at[e])

    def sum_mp():
        total = sums[m].astype(jnp.float32)
        for step in range(1, N_MP):
            m_copy(step).wait_recv()
            total = total + got_y[step - 1].astype(jnp.float32)
        for i in range(16):
            sent_t[i] = total[2 * i : 2 * i + 2].astype(jnp.bfloat16)
        for i in range(16):

            @pl.when(16 * f + i != u)
            def _():
                token_copy(i).start()

            @pl.when(16 * f + i == u)
            def _():
                token_local(i).start()

    def combine():
        for expert in range(EXPERTS):
            source = expert * SLICES + plane_f

            @pl.when(source != u)
            def _():
                token_arrival(expert).wait_recv()

            @pl.when(source == u)
            def _():
                pltpu.make_async_copy(sent_t.at[expert], got_t.at[expert], tr.at[expert]).wait()

            comb[pl.ds(2 * expert, 2)] = got_t[expert].astype(jnp.float32)
        column = lax.broadcasted_iota(jnp.int32, (8, 2 * EXPERTS), 1)
        token = lax.broadcasted_iota(jnp.int32, (8, 2 * EXPERTS), 0)
        expert_at = jnp.right_shift(column, 1)
        rank_at = jnp.bitwise_and(column, 1)
        seen = jnp.zeros_like(column)
        pick = jnp.zeros((8, 2 * EXPERTS), jnp.float32)
        for t in range(assign_ref.shape[0]):
            named = jnp.zeros_like(column)
            for k in range(assign_ref.shape[1]):
                named = named + jnp.where(expert_at == assign_ref[t, k], 1, 0)
            hit = jnp.where(seen == rank_at, named, 0)
            pick = jnp.where(token == t, hit.astype(jnp.float32), pick)
            seen = seen + named
        out = jnp.dot(
            pick.astype(jnp.bfloat16), comb[...].astype(jnp.bfloat16), preferred_element_type=jnp.float32
        )
        gtok_ref[...] = out[: gtok_ref.shape[0]].astype(jnp.bfloat16)

    stage_z(0)
    stage_x(0)
    stage_z(1)
    stage_y(0)
    sum_slices()
    stage_x(1)
    stage_f(0)
    stage_z(2)
    stage_c(0)
    stage_y(1)
    stage_x(2)
    sum_mp()
    stage_f(1)
    stage_z(3)
    stage_c(1)
    stage_y(2)
    stage_x(3)
    stage_f(2)
    stage_z(4)
    stage_c(2)
    stage_y(3)
    stage_x(4)
    stage_f(3)
    stage_z(5)
    stage_y(4)
    stage_x(5)
    stage_c(3)
    stage_f(4)
    combine()
    activate(1)
    activate(3)
    stage_y(5)
    stage_c(4)
    stage_f(5)
    stage_c(5)
    activate(2)

    x_all = rows[0, :, g].reshape(N_DP * SLOTS, quarter)
    gin_ref[...] = jnp.dot(gpt[...], x_all, preferred_element_type=jnp.float32).astype(jnp.bfloat16)
    dy_all = rows[1, :, g].reshape(N_DP * SLOTS, quarter)
    gout_ref[...] = jnp.dot(hdt[...], dy_all, preferred_element_type=jnp.float32).astype(jnp.bfloat16)

    for i in range(12):
        z_copy(i).wait_send()
        x_copy(i, own_16).wait_send()
        for way in range(2):
            y_copy(i, way, m).wait_send()
            y_forward(i, way, m_at[3] if way == 0 else m_at[1]).wait_send()
        c_copy(i, core).wait_send()
    for j in range(3):
        f_copy(j).wait_send()
        m_copy(j + 1).wait_send()
    for i in range(16):

        @pl.when(16 * f + i != u)
        def _():
            token_copy(i).wait_send()


def per_device(x_rows, dy_rows, w_in, w_out, counts, assign):
    model = w_in.shape[1]
    units = w_in.shape[3]
    quarter = model // QUARTERS
    w_flat = jnp.transpose(w_in[0], (1, 2, 0)).reshape(2 * units, model)
    w_down = jnp.transpose(w_out[0], (1, 0))
    bf16, f32 = jnp.bfloat16, jnp.float32
    dma = pltpu.SemaphoreType.DMA
    anywhere = pl.BlockSpec(memory_space=pl.ANY)
    vmem = pl.BlockSpec(memory_space=pltpu.VMEM)
    smem = pl.BlockSpec(memory_space=pltpu.SMEM)
    grad_in, grad_out, grad_tokens = pl.pallas_call(
        fused_kernel,
        out_shape=(
            jax.ShapeDtypeStruct((2 * units, quarter), bf16),
            jax.ShapeDtypeStruct((units, quarter), bf16),
            jax.ShapeDtypeStruct((assign.shape[0], quarter), bf16),
        ),
        in_specs=[anywhere, anywhere, anywhere, anywhere, vmem, smem],
        out_specs=(vmem, vmem, vmem),
        scratch_shapes=[
            pltpu.VMEM((2, N_DP, QUARTERS, SLOTS, quarter), bf16),
            pltpu.VMEM((2 * units, model), bf16),
            pltpu.VMEM((units, model), bf16),
            pltpu.VMEM((N_DP, 3 * units, SLOTS), f32),
            pltpu.VMEM((2 * units, N_DP * SLOTS), bf16),
            pltpu.VMEM((units, N_DP * SLOTS), bf16),
            pltpu.VMEM((SLOTS, model), bf16),
            pltpu.VMEM((3, 32, model), bf16),
            pltpu.VMEM((N_MP, 32, quarter), bf16),
            pltpu.VMEM((3, 32, quarter), bf16),
            pltpu.VMEM((16, 2, quarter), bf16),
            pltpu.VMEM((EXPERTS, 2, quarter), bf16),
            pltpu.VMEM((2 * EXPERTS, quarter), f32),
            dma((10,)),
            dma((12,)), dma((12,)),
            dma((12,)), dma((12,)),
            dma((48,)), dma((48,)),
            dma((12,)), dma((12,)),
            dma((3,)), dma((3,)),
            dma((3,)), dma((3,)),
            dma((16,)), dma((EXPERTS,)),
        ],
        compiler_params=pltpu.CompilerParams(
            collective_id=0, has_side_effects=True, vmem_limit_bytes=48 * 1024 * 1024
        ),
        cost_estimate=pl.CostEstimate(flops=5 * 10**9, bytes_accessed=10**7, transcendentals=10**6),
    )(x_rows, dy_rows, w_flat, w_down, counts, assign)
    grad_w_in = jnp.transpose(grad_in.reshape(2, units, quarter), (2, 0, 1))[None]
    grad_w_out = jnp.transpose(grad_out, (1, 0))[None]
    return grad_w_in, grad_w_out, grad_tokens


def solution(mesh):
    return jax.shard_map(
        per_device,
        mesh=mesh,
        in_specs=(
            P(("dp", "expert"), None),
            P(("dp", "expert"), None),
            P("expert", None, None, "mp"),
            P("expert", None, "mp"),
            P(("dp", "expert"), None),
            P(("dp", "expert"), None),
        ),
        out_specs=(
            P("expert", "dp", None, "mp"),
            P("expert", "dp", "mp"),
            P(("dp", "expert"), "mp"),
        ),
        check_vma=False,
    )
```

```python
import jax
import jax.numpy as jnp
from jax import lax
from jax.experimental import pallas as pl
from jax.experimental.pallas import tpu as pltpu
from jax.sharding import PartitionSpec as P

MESH = pl.DeviceIdType.MESH
N_DP = 4
N_MP = 4
SLICES = 4
EXPERTS = 16
SLOTS = 128
QUARTERS = 4
VMEM_LIMIT = 56 * 1024 * 1024

ROUNDS = (
    ((3, 0), (1, 3)),
    ((3, 1), (1, 2)),
    ((3, 2), (1, 1)),
    ((3, 3), (1, 0)),
    ((2, 0), (2, 3)),
    ((2, 1), (2, 2)),
)
WINDOW = 3
CHUNKS = tuple(chunk for pair in ROUNDS for chunk in pair)


def fused_kernel(
    x_ref, dy_ref, w_ref, wo_ref, counts_ref, assign_ref,
    gin_ref, gout_ref, gtok_ref,
    own, rows, w_in, w_out, acc, terms, gpt, hdt, parts, got_f, sums, got_y, sent_t, got_t, comb,
    load_sem, zs, zr, xs, xr, ys, yr, cs, cr, fs, fr, ms, mr, ts, tr,
):
    units = w_out.shape[0]
    model = w_in.shape[1]
    quarter = model // QUARTERS
    g = lax.axis_index("dp")
    u = lax.axis_index("expert")
    m = lax.axis_index("mp")
    core = lax.rem(u, 2)
    half_x = lax.rem(lax.div(u, 2), 2)
    f = lax.rem(u, SLICES)
    e = lax.div(u, SLICES)
    plane_f = lax.div(lax.div(u, 8), 2)
    flip_core = 1 - 2 * core
    flip_x = 2 - 4 * half_x
    f_shift = (flip_core, flip_x, flip_core + flip_x)
    left_g, right_g = lax.rem(g + N_DP - 1, N_DP), lax.rem(g + 1, N_DP)
    m_at = [lax.rem(m + step, N_MP) for step in range(N_MP)]

    own_16 = m * 32 + half_x * 16
    pair_16 = m * 32 + (1 - half_x) * 16
    share = pl.ds(pl.multiple_of(own_16, 16), 16)
    early = []
    for q in range(QUARTERS):
        cols = pl.ds(q * quarter, quarter)
        early.append(pltpu.make_async_copy(x_ref.at[share, cols], own.at[0, q], load_sem.at[10 + q]))
        early.append(pltpu.make_async_copy(dy_ref.at[share, cols], own.at[1, q], load_sem.at[14 + q]))
    local = []
    for q in range(QUARTERS):
        cols = pl.ds(q * quarter, quarter)
        local.append(pltpu.make_async_copy(dy_ref.at[:, cols], rows.at[1, 0, q], load_sem.at[q]))
        local.append(pltpu.make_async_copy(x_ref.at[:, cols], rows.at[0, 0, q], load_sem.at[4 + q]))
    local.append(pltpu.make_async_copy(w_ref, w_in, load_sem.at[8]))
    local.append(pltpu.make_async_copy(wo_ref, w_out, load_sem.at[9]))
    for copy in early:
        copy.start()

    barrier = pltpu.get_barrier_semaphore()

    def hello(where):
        pl.semaphore_signal(barrier, inc=1, device_id=where, device_id_type=MESH)

    hello({"dp": left_g})
    hello({"dp": right_g})
    for shift in f_shift:
        hello({"expert": u + shift})
    for step in range(1, N_MP):
        hello({"mp": m_at[step]})
    for expert in range(EXPERTS):
        source = expert * SLICES + plane_f

        @pl.when(source != u)
        def _():
            hello({"expert": source})

    own_target = (plane_f == f).astype(jnp.int32)

    counts = counts_ref[...].astype(jnp.float32)
    live_rows = jnp.sum(counts, axis=1, keepdims=True)
    row_at = lax.broadcasted_iota(jnp.int32, (SLOTS, 1), 0)
    live = row_at.astype(jnp.float32) < live_rows
    for copy in early:
        copy.wait()
    for copy in local:
        copy.start()
    own_row = lax.broadcasted_iota(jnp.int32, (16, 1), 0) + own_16
    own_live = own_row.astype(jnp.float32) < live_rows
    for q in range(QUARTERS):
        dy = own[1, q]
        own[1, q] = jnp.where(own_live, dy, jnp.zeros_like(dy))

    pl.semaphore_wait(barrier, 8 + EXPERTS - own_target)

    def rcopy(src, dst, send, recv, where):
        return pltpu.make_async_remote_copy(
            src_ref=src, dst_ref=dst, send_sem=send, recv_sem=recv, device_id=where, device_id_type=MESH
        )

    def at(kind, distance, q, start, size):
        return rows.at[kind, distance, q, pl.ds(pl.multiple_of(start, 16), size)]

    def z_copy(i):
        distance, q = CHUNKS[i]
        dst = at(core, distance, q, own_16, 16)
        if distance == 3:
            return rcopy(own.at[core, q], dst, zs.at[i], zr.at[i], {"dp": right_g})
        if distance == 1:
            return rcopy(own.at[core, q], dst, zs.at[i], zr.at[i], {"dp": left_g})
        if q < 2:
            return rcopy(at(core, 3, q, own_16, 16), dst, zs.at[i], zr.at[i], {"dp": right_g})
        return rcopy(at(core, 1, q, own_16, 16), dst, zs.at[i], zr.at[i], {"dp": left_g})

    def x_copy(i, start):
        d, q = CHUNKS[i]
        block = at(core, d, q, start, 16)
        return rcopy(block, block, xs.at[i], xr.at[i], {"expert": u + flip_x})

    def y_copy(i, way, block_m):
        d, q = CHUNKS[i]
        block = at(core, d, q, block_m * 32, 32)
        j = 4 * i + way
        return rcopy(block, block, ys.at[j], yr.at[j], {"mp": m_at[1] if way == 0 else m_at[3]})

    def y_forward(i, way, block_m):
        d, q = CHUNKS[i]
        block = at(core, d, q, block_m * 32 + 16 * way, 16)
        j = 4 * i + 2 + way
        return rcopy(block, block, ys.at[j], yr.at[j], {"mp": m_at[1] if way == 0 else m_at[3]})

    def c_copy(i, kind):
        d, q = CHUNKS[i]
        block = rows.at[kind, d, q]
        return rcopy(block, block, cs.at[i], cr.at[i], {"expert": u + flip_core})

    for i in range(2 * WINDOW):
        z_copy(i).start()

    def stage_z(k):
        for i in (2 * k, 2 * k + 1):
            z_copy(i).wait_recv()
            if k + WINDOW < len(ROUNDS):
                z_copy(i + 2 * WINDOW).start()
            x_copy(i, own_16).start()

    def stage_x(k):
        for i in (2 * k, 2 * k + 1):
            x_copy(i, pair_16).wait_recv()
            for way in range(2):
                y_copy(i, way, m).start()

    def stage_y(k):
        for i in (2 * k, 2 * k + 1):
            y_copy(i, 0, m_at[3]).wait_recv()
            y_forward(i, 0, m_at[3]).start()
            y_copy(i, 1, m_at[1]).wait_recv()
            y_forward(i, 1, m_at[1]).start()

    def stage_f(k):
        for i in (2 * k, 2 * k + 1):
            for way in range(2):
                y_forward(i, way, m_at[2]).wait_recv()
            c_copy(i, core).start()

    def multiply(d, q):
        cols = pl.ds(q * quarter, quarter)
        pre = lax.dot_general(
            w_in[:, cols], rows[0, d, q], (((1,), (1,)), ((), ())), preferred_element_type=jnp.float32
        )
        grad = lax.dot_general(
            w_out[:, cols], rows[1, d, q], (((1,), (1,)), ((), ())), preferred_element_type=jnp.float32
        )
        return pre, grad

    def stage_c(k):
        for i in (2 * k, 2 * k + 1):
            c_copy(i, 1 - core).wait_recv()
            d, q = CHUNKS[i]
            pre, grad = multiply(d, q)
            first = i < 2 or i == 8
            if first:
                acc[d, : 2 * units] = pre
                acc[d, 2 * units :] = grad
            else:
                acc[d, : 2 * units] += pre
                acc[d, 2 * units :] += grad

    def activate(d):
        gate = acc[d, :units]
        up = acc[d, units : 2 * units]
        grad = acc[d, 2 * units :]
        sigmoid = jax.nn.sigmoid(gate)
        lanes = pl.ds(d * SLOTS, SLOTS)
        hdt[:, lanes] = (gate * sigmoid * up).astype(jnp.bfloat16)
        gpt[:units, lanes] = (grad * up * sigmoid * (1.0 + gate * (1.0 - sigmoid))).astype(jnp.bfloat16)
        gpt[units:, lanes] = (grad * gate * sigmoid).astype(jnp.bfloat16)

    for q in range(QUARTERS):
        local[2 * q].wait()
        dy = rows[1, 0, q]
        rows[1, 0, q] = jnp.where(live, dy, jnp.zeros_like(dy))
        local[2 * q + 1].wait()
    local[8].wait()
    local[9].wait()
    for q in range(QUARTERS):
        pre, grad = multiply(0, q)
        if q == 0:
            acc[0, : 2 * units] = pre
            acc[0, 2 * units :] = grad
        else:
            acc[0, : 2 * units] += pre
            acc[0, 2 * units :] += grad
    activate(0)

    place = lax.broadcasted_iota(jnp.int32, (SLOTS, 1), 0)
    owner = jnp.right_shift(lax.broadcasted_iota(jnp.int32, (SLOTS, 64), 0), 1)
    other = lax.broadcasted_iota(jnp.int32, (SLOTS, 64), 1)
    spread = jnp.broadcast_to(counts, (SLOTS, 64))
    zero = jnp.zeros_like(spread)
    start = jnp.sum(jnp.where(other < owner, spread, zero), axis=1, keepdims=True)
    held = jnp.sum(jnp.where(other == owner, spread, zero), axis=1, keepdims=True)
    rank = jnp.bitwise_and(place, 1).astype(jnp.float32)
    wanted = jnp.where(rank < held, start + rank, -1.0)
    slot_at = lax.broadcasted_iota(jnp.int32, (SLOTS, SLOTS), 1).astype(jnp.float32)
    order = jnp.where(slot_at == wanted, 1.0, 0.0).astype(jnp.bfloat16)
    ordered = lax.dot_general(
        order, gpt[:, :SLOTS], (((1,), (1,)), ((), ())), preferred_element_type=jnp.float32
    ).astype(jnp.bfloat16)
    for q in range(QUARTERS):
        cols = pl.ds(q * quarter, quarter)
        parts[:, cols] = jnp.dot(ordered, w_in[:, cols], preferred_element_type=jnp.float32).astype(
            jnp.bfloat16
        )

    def f_copy(j):
        target = f + f_shift[j]
        src = parts.at[pl.ds(pl.multiple_of(target * 32, 32), 32)]
        return rcopy(src, got_f.at[j], fs.at[j], fr.at[j], {"expert": u + f_shift[j]})

    for j in range(3):
        f_copy(j).start()

    def sum_slices():
        for j in range(3):
            f_copy(j).wait_recv()
        mine = pl.ds(pl.multiple_of(f * 32, 32), 32)
        for q in range(QUARTERS):
            cols = pl.ds(q * quarter, quarter)
            total = parts[mine, cols].astype(jnp.float32)
            for j in range(3):
                total = total + got_f[j, :, cols].astype(jnp.float32)
            sums[q] = total.astype(jnp.bfloat16)
        for step in range(1, N_MP):
            m_copy(step).start()

    def m_copy(step):
        return rcopy(
            sums.at[m_at[step]], got_y.at[step - 1], ms.at[step - 1], mr.at[step - 1], {"mp": m_at[step]}
        )

    def token_copy(i):
        return rcopy(sent_t.at[i], got_t.at[e], ts.at[i], tr.at[e], {"expert": 16 * f + i})

    def token_arrival(expert):
        return rcopy(
            sent_t.at[expert], got_t.at[expert], ts.at[expert], tr.at[expert], {"expert": u}
        )

    def token_local(i):
        return pltpu.make_async_copy(sent_t.at[i], got_t.at[e], tr.at[e])

    def sum_mp():
        total = sums[m].astype(jnp.float32)
        for step in range(1, N_MP):
            m_copy(step).wait_recv()
            total = total + got_y[step - 1].astype(jnp.float32)
        for i in range(16):
            sent_t[i] = total[2 * i : 2 * i + 2].astype(jnp.bfloat16)
        for i in range(16):

            @pl.when(16 * f + i != u)
            def _():
                token_copy(i).start()

            @pl.when(16 * f + i == u)
            def _():
                token_local(i).start()

    def combine():
        for expert in range(EXPERTS):
            source = expert * SLICES + plane_f

            @pl.when(source != u)
            def _():
                token_arrival(expert).wait_recv()

            @pl.when(source == u)
            def _():
                pltpu.make_async_copy(sent_t.at[expert], got_t.at[expert], tr.at[expert]).wait()

            comb[pl.ds(2 * expert, 2)] = got_t[expert].astype(jnp.float32)
        column = lax.broadcasted_iota(jnp.int32, (8, 2 * EXPERTS), 1)
        token = lax.broadcasted_iota(jnp.int32, (8, 2 * EXPERTS), 0)
        expert_at = jnp.right_shift(column, 1)
        rank_at = jnp.bitwise_and(column, 1)
        seen = jnp.zeros_like(column)
        pick = jnp.zeros((8, 2 * EXPERTS), jnp.float32)
        for t in range(assign_ref.shape[0]):
            named = jnp.zeros_like(column)
            for k in range(assign_ref.shape[1]):
                named = named + jnp.where(expert_at == assign_ref[t, k], 1, 0)
            hit = jnp.where(seen == rank_at, named, 0)
            pick = jnp.where(token == t, hit.astype(jnp.float32), pick)
            seen = seen + named
        out = jnp.dot(
            pick.astype(jnp.bfloat16), comb[...].astype(jnp.bfloat16), preferred_element_type=jnp.float32
        )
        gtok_ref[...] = out[: gtok_ref.shape[0]].astype(jnp.bfloat16)

    def sum_terms(part):
        two = pl.ds(2 * part, 2)
        lanes = pl.ds(2 * part * SLOTS, 2 * SLOTS)
        x_two = rows[0, two, g].reshape(2 * SLOTS, quarter)
        dy_two = rows[1, two, g].reshape(2 * SLOTS, quarter)
        g_in = jnp.dot(gpt[:, lanes], x_two, preferred_element_type=jnp.float32)
        g_out = jnp.dot(hdt[:, lanes], dy_two, preferred_element_type=jnp.float32)
        if part == 0:
            terms[: 2 * units] = g_in
            terms[2 * units :] = g_out
        else:
            gin_ref[...] = (terms[: 2 * units] + g_in).astype(jnp.bfloat16)
            gout_ref[...] = (terms[2 * units :] + g_out).astype(jnp.bfloat16)

    def sent(k):
        for i in (2 * k, 2 * k + 1):
            z_copy(i).wait_send()
            x_copy(i, own_16).wait_send()
            for way in range(2):
                y_copy(i, way, m).wait_send()
                y_forward(i, way, m_at[3] if way == 0 else m_at[1]).wait_send()
            c_copy(i, core).wait_send()

    def rows_sent():
        for j in range(3):
            f_copy(j).wait_send()
            m_copy(j + 1).wait_send()
        for i in range(16):

            @pl.when(16 * f + i != u)
            def _():
                token_copy(i).wait_send()

    last = len(ROUNDS)
    for t in range(last + 4):
        if t < last:
            stage_z(t)
        if 1 <= t <= last:
            stage_x(t - 1)
        if 2 <= t <= last + 1:
            stage_y(t - 2)
        if 3 <= t <= last + 2:
            stage_f(t - 3)
        if t == 1:
            sum_slices()
        if t == 3:
            sum_mp()
        if t == last - 1:
            combine()
        if t == last:
            rows_sent()
        if t >= 4:
            stage_c(t - 4)
        if t == last + 1:
            activate(1)
            activate(3)
            sum_terms(0)
        if t >= 5 and t - 5 < last - 2:
            sent(t - 5)
    activate(2)

    sum_terms(1)

    sent(last - 2)
    sent(last - 1)


def copy_kernel(a_in, b_in, c_in, a_out, b_out, c_out, a_held, b_held, c_held, in_sem, out_sem):
    held = (a_held, b_held, c_held)
    reads = [pltpu.make_async_copy(src, held[i], in_sem.at[i]) for i, src in enumerate((a_in, b_in, c_in))]
    writes = [pltpu.make_async_copy(held[i], dst, out_sem.at[i]) for i, dst in enumerate((a_out, b_out, c_out))]
    for copy in reads:
        copy.start()
    for read, write in zip(reads, writes):
        read.wait()
        write.start()
    for copy in writes:
        copy.wait()


def per_device(x_rows, dy_rows, w_in, w_out, counts, assign):
    model = w_in.shape[1]
    units = w_in.shape[3]
    quarter = model // QUARTERS
    w_flat = jnp.transpose(w_in[0], (1, 2, 0)).reshape(2 * units, model)
    w_down = jnp.transpose(w_out[0], (1, 0))
    bf16, f32 = jnp.bfloat16, jnp.float32
    dma = pltpu.SemaphoreType.DMA
    anywhere = pl.BlockSpec(memory_space=pltpu.HBM)
    vmem = pl.BlockSpec(memory_space=pltpu.VMEM)
    smem = pl.BlockSpec(memory_space=pltpu.SMEM)
    held = pl.pallas_call(
        fused_kernel,
        out_shape=(
            jax.ShapeDtypeStruct((2 * units, quarter), bf16),
            jax.ShapeDtypeStruct((units, quarter), bf16),
            jax.ShapeDtypeStruct((assign.shape[0], quarter), bf16),
        ),
        in_specs=[anywhere, anywhere, anywhere, anywhere, vmem, smem],
        out_specs=(vmem, vmem, vmem),
        scratch_shapes=[
            pltpu.VMEM((2, QUARTERS, 16, quarter), bf16),
            pltpu.VMEM((2, N_DP, QUARTERS, SLOTS, quarter), bf16),
            pltpu.VMEM((2 * units, model), bf16),
            pltpu.VMEM((units, model), bf16),
            pltpu.VMEM((N_DP, 3 * units, SLOTS), f32),
            pltpu.VMEM((3 * units, quarter), f32),
            pltpu.VMEM((2 * units, N_DP * SLOTS), bf16),
            pltpu.VMEM((units, N_DP * SLOTS), bf16),
            pltpu.VMEM((SLOTS, model), bf16),
            pltpu.VMEM((3, 32, model), bf16),
            pltpu.VMEM((N_MP, 32, quarter), bf16),
            pltpu.VMEM((3, 32, quarter), bf16),
            pltpu.VMEM((16, 2, quarter), bf16),
            pltpu.VMEM((EXPERTS, 2, quarter), bf16),
            pltpu.VMEM((2 * EXPERTS, quarter), f32),
            dma((18,)),
            dma((12,)), dma((12,)),
            dma((12,)), dma((12,)),
            dma((48,)), dma((48,)),
            dma((48,)), dma((48,)),
            dma((3,)), dma((3,)),
            dma((3,)), dma((3,)),
            dma((16,)), dma((EXPERTS,)),
        ],
        compiler_params=pltpu.CompilerParams(
            collective_id=0, has_side_effects=True, vmem_limit_bytes=VMEM_LIMIT
        ),
        cost_estimate=pl.CostEstimate(flops=5 * 10**9, bytes_accessed=10**7, transcendentals=10**6),
    )(x_rows, dy_rows, w_flat, w_down, counts, assign)
    shapes = tuple(jax.ShapeDtypeStruct(part.shape, part.dtype) for part in held)
    grad_in, grad_out, grad_tokens = pl.pallas_call(
        copy_kernel,
        out_shape=shapes,
        in_specs=[anywhere] * 3,
        out_specs=(anywhere,) * 3,
        scratch_shapes=[pltpu.VMEM(part.shape, part.dtype) for part in shapes] + [dma((3,)), dma((3,))],
        compiler_params=pltpu.CompilerParams(vmem_limit_bytes=VMEM_LIMIT),
    )(*held)
    grad_w_in = jnp.transpose(grad_in.reshape(2, units, quarter), (2, 0, 1))[None]
    grad_w_out = jnp.transpose(grad_out, (1, 0))[None]
    return grad_w_in, grad_w_out, grad_tokens


def solution(mesh):
    return jax.shard_map(
        per_device,
        mesh=mesh,
        in_specs=(
            P(("dp", "expert"), None),
            P(("dp", "expert"), None),
            P("expert", None, None, "mp"),
            P("expert", None, "mp"),
            P(("dp", "expert"), None),
            P(("dp", "expert"), None),
        ),
        out_specs=(
            P("expert", "dp", None, "mp"),
            P("expert", "dp", "mp"),
            P(("dp", "expert"), "mp"),
        ),
        check_vma=False,
    )
```

```python
import jax
import jax.numpy as jnp
from jax import lax
from jax.experimental import pallas as pl
from jax.experimental.pallas import tpu as pltpu
from jax.sharding import PartitionSpec as P

MESH = pl.DeviceIdType.MESH
N_DP = 4
N_MP = 4
SLICES = 4
EXPERTS = 16
SLOTS = 128
QUARTERS = 4
VMEM_LIMIT = 54 * 1024 * 1024

ROUNDS = (
    ((3, 0), (1, 3)),
    ((3, 1), (1, 2)),
    ((3, 2), (1, 1)),
    ((3, 3), (1, 0)),
    ((2, 0), (2, 3)),
    ((2, 1), (2, 2)),
)
WINDOW = 3
CHUNKS = tuple(chunk for pair in ROUNDS for chunk in pair)


def fused_kernel(
    x_ref, dy_ref, w_ref, wo_ref, counts_ref, assign_ref,
    gin_ref, gout_ref, gtok_ref,
    own, rows, w_in, w_out, acc, terms, gpt, hdt, parts, got_f, sums, got_y, sent_t, got_t, comb,
    load_sem, zs, zr, xs, xr, ys, yr, cs, cr, fs, fr, ms, mr, ts, tr,
):
    units = w_out.shape[0]
    model = w_in.shape[1]
    quarter = model // QUARTERS
    g = lax.axis_index("dp")
    u = lax.axis_index("expert")
    m = lax.axis_index("mp")
    core = lax.rem(u, 2)
    half_x = lax.rem(lax.div(u, 2), 2)
    f = lax.rem(u, SLICES)
    e = lax.div(u, SLICES)
    plane_f = lax.div(lax.div(u, 8), 2)
    flip_core = 1 - 2 * core
    flip_x = 2 - 4 * half_x
    f_shift = (flip_core, flip_x, flip_core + flip_x)
    left_g, right_g = lax.rem(g + N_DP - 1, N_DP), lax.rem(g + 1, N_DP)
    m_at = [lax.rem(m + step, N_MP) for step in range(N_MP)]

    own_16 = m * 32 + half_x * 16
    pair_16 = m * 32 + (1 - half_x) * 16
    share = pl.ds(pl.multiple_of(own_16, 16), 16)
    early = []
    for q in range(QUARTERS):
        cols = pl.ds(q * quarter, quarter)
        early.append(pltpu.make_async_copy(x_ref.at[share, cols], own.at[0, q], load_sem.at[10 + q]))
        early.append(pltpu.make_async_copy(dy_ref.at[share, cols], own.at[1, q], load_sem.at[14 + q]))
    local = []
    for q in range(QUARTERS):
        cols = pl.ds(q * quarter, quarter)
        local.append(pltpu.make_async_copy(dy_ref.at[:, cols], rows.at[1, 0, q], load_sem.at[q]))
        local.append(pltpu.make_async_copy(x_ref.at[:, cols], rows.at[0, 0, q], load_sem.at[4 + q]))
    local.append(pltpu.make_async_copy(w_ref, w_in, load_sem.at[8]))
    local.append(pltpu.make_async_copy(wo_ref, w_out, load_sem.at[9]))
    for copy in early:
        copy.start()

    barrier = pltpu.get_barrier_semaphore()

    def hello(where):
        pl.semaphore_signal(barrier, inc=1, device_id=where, device_id_type=MESH)

    hello({"dp": left_g})
    hello({"dp": right_g})
    for shift in f_shift:
        hello({"expert": u + shift})
    for step in range(1, N_MP):
        hello({"mp": m_at[step]})
    for expert in range(EXPERTS):
        source = expert * SLICES + plane_f

        @pl.when(source != u)
        def _():
            hello({"expert": source})

    own_target = (plane_f == f).astype(jnp.int32)

    counts = counts_ref[...].astype(jnp.float32)
    live_rows = jnp.sum(counts, axis=1, keepdims=True)
    row_at = lax.broadcasted_iota(jnp.int32, (SLOTS, 1), 0)
    live = row_at.astype(jnp.float32) < live_rows
    for copy in early:
        copy.wait()
    for copy in local:
        copy.start()
    own_row = lax.broadcasted_iota(jnp.int32, (16, 1), 0) + own_16
    own_live = own_row.astype(jnp.float32) < live_rows
    for q in range(QUARTERS):
        dy = own[1, q]
        own[1, q] = jnp.where(own_live, dy, jnp.zeros_like(dy))

    pl.semaphore_wait(barrier, 8 + EXPERTS - own_target)

    def rcopy(src, dst, send, recv, where):
        return pltpu.make_async_remote_copy(
            src_ref=src, dst_ref=dst, send_sem=send, recv_sem=recv, device_id=where, device_id_type=MESH
        )

    def at(kind, distance, q, start, size):
        return rows.at[kind, distance, q, pl.ds(pl.multiple_of(start, 16), size)]

    def z_copy(i):
        distance, q = CHUNKS[i]
        dst = at(core, distance, q, own_16, 16)
        if distance == 3:
            return rcopy(own.at[core, q], dst, zs.at[i], zr.at[i], {"dp": right_g})
        if distance == 1:
            return rcopy(own.at[core, q], dst, zs.at[i], zr.at[i], {"dp": left_g})
        if q < 2:
            return rcopy(at(core, 3, q, own_16, 16), dst, zs.at[i], zr.at[i], {"dp": right_g})
        return rcopy(at(core, 1, q, own_16, 16), dst, zs.at[i], zr.at[i], {"dp": left_g})

    def x_copy(i, start):
        d, q = CHUNKS[i]
        block = at(core, d, q, start, 16)
        return rcopy(block, block, xs.at[i], xr.at[i], {"expert": u + flip_x})

    def y_copy(i, way, block_m, side):
        d, q = CHUNKS[i]
        block = at(core, d, q, block_m * 32 + 16 * side, 16)
        j = 2 * way + side
        return rcopy(block, block, ys.at[i, j], yr.at[i, j], {"mp": m_at[1] if way == 0 else m_at[3]})

    def y_forward(i, way, block_m):
        d, q = CHUNKS[i]
        block = at(core, d, q, block_m * 32 + 16 * way, 16)
        j = 4 + way
        return rcopy(block, block, ys.at[i, j], yr.at[i, j], {"mp": m_at[1] if way == 0 else m_at[3]})

    def c_copy(i, kind):
        d, q = CHUNKS[i]
        block = rows.at[kind, d, q]
        return rcopy(block, block, cs.at[i], cr.at[i], {"expert": u + flip_core})

    for i in range(2 * WINDOW):
        z_copy(i).start()

    def stage_z(k):
        for i in (2 * k, 2 * k + 1):
            z_copy(i).wait_recv()
            if k + WINDOW < len(ROUNDS):
                z_copy(i + 2 * WINDOW).start()
            x_copy(i, own_16).start()
            for way in range(2):
                y_copy(i, way, m, half_x).start()

    def stage_x(k):
        for i in (2 * k, 2 * k + 1):
            x_copy(i, pair_16).wait_recv()
            for way in range(2):
                y_copy(i, way, m, 1 - half_x).start()

    def stage_y(k):
        for i in (2 * k, 2 * k + 1):
            y_copy(i, 0, m_at[3], half_x).wait_recv()
            y_copy(i, 0, m_at[3], 1 - half_x).wait_recv()
            y_forward(i, 0, m_at[3]).start()
            y_copy(i, 1, m_at[1], half_x).wait_recv()
            y_copy(i, 1, m_at[1], 1 - half_x).wait_recv()
            y_forward(i, 1, m_at[1]).start()

    def stage_f(k):
        for i in (2 * k, 2 * k + 1):
            for way in range(2):
                y_forward(i, way, m_at[2]).wait_recv()
            c_copy(i, core).start()

    def multiply(d, q):
        cols = pl.ds(q * quarter, quarter)
        pre = lax.dot_general(
            w_in[:, cols], rows[0, d, q], (((1,), (1,)), ((), ())), preferred_element_type=jnp.float32
        )
        grad = lax.dot_general(
            w_out[:, cols], rows[1, d, q], (((1,), (1,)), ((), ())), preferred_element_type=jnp.float32
        )
        return pre, grad

    def stage_c(k):
        for i in (2 * k, 2 * k + 1):
            c_copy(i, 1 - core).wait_recv()
            d, q = CHUNKS[i]
            pre, grad = multiply(d, q)
            first = i < 2 or i == 8
            if first:
                acc[d, : 2 * units] = pre
                acc[d, 2 * units :] = grad
            else:
                acc[d, : 2 * units] += pre
                acc[d, 2 * units :] += grad

    def activate(d):
        gate = acc[d, :units]
        up = acc[d, units : 2 * units]
        grad = acc[d, 2 * units :]
        sigmoid = jax.nn.sigmoid(gate)
        lanes = pl.ds(d * SLOTS, SLOTS)
        hdt[:, lanes] = (gate * sigmoid * up).astype(jnp.bfloat16)
        gpt[:units, lanes] = (grad * up * sigmoid * (1.0 + gate * (1.0 - sigmoid))).astype(jnp.bfloat16)
        gpt[units:, lanes] = (grad * gate * sigmoid).astype(jnp.bfloat16)

    for q in range(QUARTERS):
        local[2 * q].wait()
        dy = rows[1, 0, q]
        rows[1, 0, q] = jnp.where(live, dy, jnp.zeros_like(dy))
        local[2 * q + 1].wait()
    local[8].wait()
    local[9].wait()
    for q in range(QUARTERS):
        pre, grad = multiply(0, q)
        if q == 0:
            acc[0, : 2 * units] = pre
            acc[0, 2 * units :] = grad
        else:
            acc[0, : 2 * units] += pre
            acc[0, 2 * units :] += grad
    activate(0)

    place = lax.broadcasted_iota(jnp.int32, (SLOTS, 1), 0)
    owner = jnp.right_shift(lax.broadcasted_iota(jnp.int32, (SLOTS, 64), 0), 1)
    other = lax.broadcasted_iota(jnp.int32, (SLOTS, 64), 1)
    spread = jnp.broadcast_to(counts, (SLOTS, 64))
    zero = jnp.zeros_like(spread)
    start = jnp.sum(jnp.where(other < owner, spread, zero), axis=1, keepdims=True)
    held = jnp.sum(jnp.where(other == owner, spread, zero), axis=1, keepdims=True)
    rank = jnp.bitwise_and(place, 1).astype(jnp.float32)
    wanted = jnp.where(rank < held, start + rank, -1.0)
    slot_at = lax.broadcasted_iota(jnp.int32, (SLOTS, SLOTS), 1).astype(jnp.float32)
    order = jnp.where(slot_at == wanted, 1.0, 0.0).astype(jnp.bfloat16)
    ordered = lax.dot_general(
        order, gpt[:, :SLOTS], (((1,), (1,)), ((), ())), preferred_element_type=jnp.float32
    ).astype(jnp.bfloat16)
    for q in range(QUARTERS):
        cols = pl.ds(q * quarter, quarter)
        parts[:, cols] = jnp.dot(ordered, w_in[:, cols], preferred_element_type=jnp.float32).astype(
            jnp.bfloat16
        )

    def f_copy(j):
        target = f + f_shift[j]
        src = parts.at[pl.ds(pl.multiple_of(target * 32, 32), 32)]
        return rcopy(src, got_f.at[j], fs.at[j], fr.at[j], {"expert": u + f_shift[j]})

    for j in range(3):
        f_copy(j).start()

    def sum_slices():
        for j in range(3):
            f_copy(j).wait_recv()
        mine = pl.ds(pl.multiple_of(f * 32, 32), 32)
        for q in range(QUARTERS):
            cols = pl.ds(q * quarter, quarter)
            total = parts[mine, cols].astype(jnp.float32)
            for j in range(3):
                total = total + got_f[j, :, cols].astype(jnp.float32)
            sums[q] = total.astype(jnp.bfloat16)
        for step in range(1, N_MP):
            m_copy(step).start()

    def m_copy(step):
        return rcopy(
            sums.at[m_at[step]], got_y.at[step - 1], ms.at[step - 1], mr.at[step - 1], {"mp": m_at[step]}
        )

    def token_copy(i):
        return rcopy(sent_t.at[i], got_t.at[e], ts.at[i], tr.at[e], {"expert": 16 * f + i})

    def token_arrival(expert):
        return rcopy(
            sent_t.at[expert], got_t.at[expert], ts.at[expert], tr.at[expert], {"expert": u}
        )

    def token_local(i):
        return pltpu.make_async_copy(sent_t.at[i], got_t.at[e], tr.at[e])

    def sum_mp():
        total = sums[m].astype(jnp.float32)
        for step in range(1, N_MP):
            m_copy(step).wait_recv()
            total = total + got_y[step - 1].astype(jnp.float32)
        for i in range(16):
            sent_t[i] = total[2 * i : 2 * i + 2].astype(jnp.bfloat16)
        for i in range(16):

            @pl.when(16 * f + i != u)
            def _():
                token_copy(i).start()

            @pl.when(16 * f + i == u)
            def _():
                token_local(i).start()

    def combine():
        for expert in range(EXPERTS):
            source = expert * SLICES + plane_f

            @pl.when(source != u)
            def _():
                token_arrival(expert).wait_recv()

            @pl.when(source == u)
            def _():
                pltpu.make_async_copy(sent_t.at[expert], got_t.at[expert], tr.at[expert]).wait()

            comb[pl.ds(2 * expert, 2)] = got_t[expert].astype(jnp.float32)
        column = lax.broadcasted_iota(jnp.int32, (8, 2 * EXPERTS), 1)
        token = lax.broadcasted_iota(jnp.int32, (8, 2 * EXPERTS), 0)
        expert_at = jnp.right_shift(column, 1)
        rank_at = jnp.bitwise_and(column, 1)
        seen = jnp.zeros_like(column)
        pick = jnp.zeros((8, 2 * EXPERTS), jnp.float32)
        for t in range(assign_ref.shape[0]):
            named = jnp.zeros_like(column)
            for k in range(assign_ref.shape[1]):
                named = named + jnp.where(expert_at == assign_ref[t, k], 1, 0)
            hit = jnp.where(seen == rank_at, named, 0)
            pick = jnp.where(token == t, hit.astype(jnp.float32), pick)
            seen = seen + named
        out = jnp.dot(
            pick.astype(jnp.bfloat16), comb[...].astype(jnp.bfloat16), preferred_element_type=jnp.float32
        )
        gtok_ref[...] = out[: gtok_ref.shape[0]].astype(jnp.bfloat16)

    def sum_terms(part):
        two = pl.ds(2 * part, 2)
        lanes = pl.ds(2 * part * SLOTS, 2 * SLOTS)
        x_two = rows[0, two, g].reshape(2 * SLOTS, quarter)
        dy_two = rows[1, two, g].reshape(2 * SLOTS, quarter)
        g_in = jnp.dot(gpt[:, lanes], x_two, preferred_element_type=jnp.float32)
        g_out = jnp.dot(hdt[:, lanes], dy_two, preferred_element_type=jnp.float32)
        if part == 0:
            terms[: 2 * units] = g_in
            terms[2 * units :] = g_out
        else:
            gin_ref[...] = (terms[: 2 * units] + g_in).astype(jnp.bfloat16)
            gout_ref[...] = (terms[2 * units :] + g_out).astype(jnp.bfloat16)

    def sent(k):
        for i in (2 * k, 2 * k + 1):
            z_copy(i).wait_send()
            x_copy(i, own_16).wait_send()
            for way in range(2):
                for side in range(2):
                    y_copy(i, way, m, side).wait_send()
                y_forward(i, way, m_at[3] if way == 0 else m_at[1]).wait_send()
            c_copy(i, core).wait_send()

    def rows_sent():
        for j in range(3):
            f_copy(j).wait_send()
            m_copy(j + 1).wait_send()
        for i in range(16):

            @pl.when(16 * f + i != u)
            def _():
                token_copy(i).wait_send()

    last = len(ROUNDS)
    for t in range(last + 4):
        if t < last:
            stage_z(t)
        if 1 <= t <= last:
            stage_x(t - 1)
        if 2 <= t <= last + 1:
            stage_y(t - 2)
        if 3 <= t <= last + 2:
            stage_f(t - 3)
        if t == 1:
            sum_slices()
        if t == 3:
            sum_mp()
        if t == last - 1:
            combine()
        if t == last:
            rows_sent()
        if t >= 4:
            stage_c(t - 4)
        if t == last + 1:
            activate(1)
            activate(3)
            sum_terms(0)
        if t >= 5 and t - 5 < last - 2:
            sent(t - 5)
    activate(2)

    sum_terms(1)

    sent(last - 2)
    sent(last - 1)


def copy_kernel(a_in, b_in, c_in, a_out, b_out, c_out, a_held, b_held, c_held, in_sem, out_sem):
    pieces = []
    for src, held, dst in ((a_in, a_held, a_out), (b_in, b_held, b_out)):
        size = 112
        for first in range(0, src.shape[0], size):
            cut = pl.ds(first, size)
            pieces.append((src.at[cut], held.at[cut], dst.at[cut]))
    pieces.append((c_in, c_held, c_out))
    reads = [pltpu.make_async_copy(src, held, in_sem.at[i]) for i, (src, held, _) in enumerate(pieces)]
    writes = [pltpu.make_async_copy(held, dst, out_sem.at[i]) for i, (_, held, dst) in enumerate(pieces)]
    for copy in reads:
        copy.start()
    for read, write in zip(reads, writes):
        read.wait()
        write.start()
    for copy in writes:
        copy.wait()


def per_device(x_rows, dy_rows, w_in, w_out, counts, assign):
    model = w_in.shape[1]
    units = w_in.shape[3]
    quarter = model // QUARTERS
    w_flat = jnp.transpose(w_in[0], (1, 2, 0)).reshape(2 * units, model)
    w_down = jnp.transpose(w_out[0], (1, 0))
    bf16, f32 = jnp.bfloat16, jnp.float32
    dma = pltpu.SemaphoreType.DMA
    anywhere = pl.BlockSpec(memory_space=pltpu.HBM)
    vmem = pl.BlockSpec(memory_space=pltpu.VMEM)
    smem = pl.BlockSpec(memory_space=pltpu.SMEM)
    held = pl.pallas_call(
        fused_kernel,
        out_shape=(
            jax.ShapeDtypeStruct((2 * units, quarter), bf16),
            jax.ShapeDtypeStruct((units, quarter), bf16),
            jax.ShapeDtypeStruct((assign.shape[0], quarter), bf16),
        ),
        in_specs=[anywhere, anywhere, anywhere, anywhere, vmem, smem],
        out_specs=(vmem, vmem, vmem),
        scratch_shapes=[
            pltpu.VMEM((2, QUARTERS, 16, quarter), bf16),
            pltpu.VMEM((2, N_DP, QUARTERS, SLOTS, quarter), bf16),
            pltpu.VMEM((2 * units, model), bf16),
            pltpu.VMEM((units, model), bf16),
            pltpu.VMEM((N_DP, 3 * units, SLOTS), f32),
            pltpu.VMEM((3 * units, quarter), f32),
            pltpu.VMEM((2 * units, N_DP * SLOTS), bf16),
            pltpu.VMEM((units, N_DP * SLOTS), bf16),
            pltpu.VMEM((SLOTS, model), bf16),
            pltpu.VMEM((3, 32, model), bf16),
            pltpu.VMEM((N_MP, 32, quarter), bf16),
            pltpu.VMEM((3, 32, quarter), bf16),
            pltpu.VMEM((16, 2, quarter), bf16),
            pltpu.VMEM((EXPERTS, 2, quarter), bf16),
            pltpu.VMEM((2 * EXPERTS, quarter), f32),
            dma((18,)),
            dma((12,)), dma((12,)),
            dma((12,)), dma((12,)),
            dma((12, 6)), dma((12, 6)),
            dma((48,)), dma((48,)),
            dma((3,)), dma((3,)),
            dma((3,)), dma((3,)),
            dma((16,)), dma((EXPERTS,)),
        ],
        compiler_params=pltpu.CompilerParams(
            collective_id=0, has_side_effects=True, vmem_limit_bytes=VMEM_LIMIT
        ),
        cost_estimate=pl.CostEstimate(flops=5 * 10**9, bytes_accessed=10**7, transcendentals=10**6),
    )(x_rows, dy_rows, w_flat, w_down, counts, assign)
    shapes = tuple(jax.ShapeDtypeStruct(part.shape, part.dtype) for part in held)
    grad_in, grad_out, grad_tokens = pl.pallas_call(
        copy_kernel,
        out_shape=shapes,
        in_specs=[anywhere] * 3,
        out_specs=(anywhere,) * 3,
        scratch_shapes=[pltpu.VMEM(part.shape, part.dtype) for part in shapes] + [dma((10,)), dma((10,))],
        compiler_params=pltpu.CompilerParams(vmem_limit_bytes=VMEM_LIMIT),
    )(*held)
    grad_w_in = jnp.transpose(grad_in.reshape(2, units, quarter), (2, 0, 1))[None]
    grad_w_out = jnp.transpose(grad_out, (1, 0))[None]
    return grad_w_in, grad_w_out, grad_tokens


def solution(mesh):
    return jax.shard_map(
        per_device,
        mesh=mesh,
        in_specs=(
            P(("dp", "expert"), None),
            P(("dp", "expert"), None),
            P("expert", None, None, "mp"),
            P("expert", None, "mp"),
            P(("dp", "expert"), None),
            P(("dp", "expert"), None),
        ),
        out_specs=(
            P("expert", "dp", None, "mp"),
            P("expert", "dp", "mp"),
            P(("dp", "expert"), "mp"),
        ),
        check_vma=False,
    )
```
